32 devices in a mesh: ctx: 8 (over z, x), head: 4 (over y, core).
Axes of the slice: x: 2, y: 2, z: 4, core: 2. Of those that a mesh axis runs over, the one named last changes fastest.
Arguments:
- queries: bfloat16 [1024, 4096], P('ctx', 'head'), may hold values from -5 to 5
- keys: bfloat16 [1024, 4096], P('ctx', 'head'), may hold values from -5 to 5
- values: bfloat16 [1024, 4096], P('ctx', 'head'), may hold values from -6 to 6
- episode: int32 [1024], P('ctx'), may hold values from 0 to 30, as said below
- out_weight: bfloat16 [4096, 4096], P('head'), may hold values from -1.5 to 1.5
- d_out: bfloat16 [1024, 4096], P(('ctx', 'head')), may hold values from -0.3984375 to 0.3984375
Outputs:
- mixed: bfloat16 [1024, 4096], P(('ctx', 'head'))
- d_queries: bfloat16 [1024, 4096], P('ctx', 'head')
- d_keys: bfloat16 [1024, 4096], P('ctx', 'head')
- d_values: bfloat16 [1024, 4096], P('ctx', 'head')
The draws below stay inside these ranges and needn't reach their ends.
Inputs may be any that keep to these rules, and one draw needn't show every extreme that they name: Episode numbers never fall as time rises; the episode of time step t is 0 for t < 64 and 2 * (t // 64) - 1 or 2 * (t // 64) otherwise (so each episode has 1 to 64 time steps, and episode 0 has exactly 64).
All inputs are finite; a program needn't handle non-finite values.
Results may differ from the reference program's by a relative error of at most 0.02.
Values may be sent and summed in bfloat16 or wider, within the bound.
A program may use at most 64 MiB of HBM per device.

```python
import jax
import jax.numpy as jnp
from jax import lax

D = 4096
H = 32
HD = 128
TOK_DEV = 128
TOKENS = 1024
WINDOW_EPS = 16
MOST = 64
N_CTX = 8


def normal_rows(key, factor):
    return jnp.clip(factor * jax.random.normal(key, (TOKENS, H * HD), jnp.float32), -5.0, 5.0)


def draw_queries(key, part):
    key = jax.random.fold_in(key, 1)
    field = normal_rows(key, 1.0)
    return field.astype(jnp.bfloat16)


def draw_keys(key, part):
    key = jax.random.fold_in(key, 2)
    field = normal_rows(key, 2.0)
    return field.astype(jnp.bfloat16)


def draw_episode(key, part):
    key = jax.random.fold_in(key, 3)
    spans = TOKENS // MOST
    cuts = jax.random.randint(key, (spans,), 1, MOST).astype(jnp.int32)
    cuts = cuts.at[0].set(MOST)
    moments = jnp.arange(TOKENS, dtype=jnp.int32)
    span_of = moments // MOST
    offset = moments % MOST
    later = (offset >= cuts[span_of]).astype(jnp.int32)
    first = (span_of >= 1).astype(jnp.int32)
    by_time = 2 * span_of + later - first
    blocks = TOKENS // TOK_DEV
    half_rows = TOK_DEV // 2
    rows = jnp.arange(TOKENS, dtype=jnp.int32)
    holder = rows // TOK_DEV
    place_in = rows % TOK_DEV
    stamps = jnp.where(place_in < half_rows, holder * half_rows + place_in, (2 * blocks - 1 - holder) * half_rows + place_in - half_rows).astype(jnp.int32)
    return by_time[stamps].astype(jnp.int32)


def levels(key, dims, cuts, low, top_value):
    factor_of, own = 1.0, jax.random.fold_in(key, 6)
    for axis_at, blocks in cuts:
        heights = jnp.exp(jax.random.uniform(jax.random.fold_in(own, axis_at), (blocks,), jnp.float32, low / len(cuts), top_value / len(cuts)))
        factor_of = factor_of * jnp.repeat(heights, dims[axis_at] // blocks).reshape([-1 if axis == axis_at else 1 for axis in range(len(dims))])
    return factor_of


def centred(rng, dims, width, limit, cuts=(), held_as=jnp.bfloat16):
    result = jax.random.normal(rng, dims, jnp.float32) * width
    if len(cuts) > 0:
        result = levels(rng, dims, cuts, -0.22, 0.18) * result
    return jnp.clip(result, min=-limit, max=limit).astype(held_as)


def setup_inputs(seed: int = 0) -> dict:
    streams_of = jax.random.split(jax.random.key(seed), 7)
    queries = draw_queries(jax.random.fold_in(streams_of[6], 71), 0)
    keys = draw_keys(jax.random.fold_in(streams_of[6], 71), 0)
    values = centred(streams_of[2], (TOKENS, H * HD), 1.0, 6.0, ((0, 8), (1, 4)))
    episode = draw_episode(jax.random.fold_in(streams_of[6], 71), 0)
    out_weight = centred(streams_of[4], (H * HD, D), 0.25, 1.5, ((0, 4),))
    d_out = centred(streams_of[5], (TOKENS, D), 0.0625, 0.3984375, ((0, 32),))
    return dict(queries=queries, keys=keys, values=values, episode=episode, out_weight=out_weight, d_out=d_out)


floor_score = -1e30


def time_steps(rows):
    half_rows = TOK_DEV // 2
    holder = rows // TOK_DEV
    offset = rows % TOK_DEV
    return jnp.where(offset < half_rows, holder * half_rows + offset,
                     (2 * N_CTX - 1 - holder) * half_rows + offset - half_rows).astype(jnp.int32)


def reference(queries, keys, values, episode, out_weight, d_out):
    scale = HD ** -0.5
    d_attn = jnp.dot(d_out, out_weight.T, preferred_element_type=jnp.float32).astype(jnp.bfloat16)
    stamps = time_steps(jnp.arange(TOKENS, dtype=jnp.int32))
    visible = (stamps[None, :] <= stamps[:, None]) & (episode[:, None] - episode[None, :] < WINDOW_EPS)

    def split_heads(array):
        return array.reshape(TOKENS, H, HD).transpose(1, 0, 2)

    def merge_heads(array):
        return array.transpose(1, 0, 2).reshape(TOKENS, H * HD)

    def one_head(operands):
        q_head, k_head, v_head, da_head = operands
        scores = jnp.dot(q_head, k_head.T, preferred_element_type=jnp.float32) * scale
        scores = jnp.where(visible, scores, floor_score)
        top = jnp.max(scores, axis=1)
        lse = top + jnp.log(jnp.sum(jnp.exp(scores - top[:, None]), axis=1))
        probs = jnp.exp(scores - lse[:, None])
        probs_low = probs.astype(jnp.bfloat16)
        attn_head = jnp.dot(probs_low, v_head, preferred_element_type=jnp.float32).astype(jnp.bfloat16)
        delta = jnp.sum(da_head.astype(jnp.float32) * attn_head.astype(jnp.float32), axis=1)
        d_probs = jnp.dot(da_head, v_head.T, preferred_element_type=jnp.float32)
        d_scores = (probs * (d_probs - delta[:, None])).astype(jnp.bfloat16)
        dq_head = (scale * jnp.dot(d_scores, k_head, preferred_element_type=jnp.float32)).astype(jnp.bfloat16)
        dk_head = (scale * jnp.dot(d_scores.T, q_head, preferred_element_type=jnp.float32)).astype(jnp.bfloat16)
        dv_head = jnp.dot(probs_low.T, da_head, preferred_element_type=jnp.float32).astype(jnp.bfloat16)
        return attn_head, dq_head, dk_head, dv_head

    attn, d_queries, d_keys, d_values = lax.map(
        one_head, (split_heads(queries), split_heads(keys), split_heads(values), split_heads(d_attn)))
    mixed = jnp.dot(merge_heads(attn), out_weight, preferred_element_type=jnp.float32).astype(jnp.bfloat16)
    return mixed, merge_heads(d_queries), merge_heads(d_keys), merge_heads(d_values)
```

```python
import jax
import jax.numpy as jnp
from jax import lax
from jax.sharding import PartitionSpec as P

HD = 128


floor_score = -1e30


def time_steps(rows, rows_local, ctx_count):
    half_rows = rows_local // 2
    holder = rows // rows_local
    offset = rows % rows_local
    return jnp.where(
        offset < half_rows,
        holder * half_rows + offset,
        (2 * ctx_count - 1 - holder) * half_rows + offset - half_rows,
    )


def on_device(queries, keys, values, episode, out_weight, d_out):
    rows_local = queries.shape[0]
    width = queries.shape[1]
    heads = width // HD
    scale = HD ** (-0.5)
    place = lax.axis_index("ctx")
    ctx_count = lax.axis_size("ctx")
    window = 2 * ctx_count
    d_attn = lax.dot_general(
        lax.all_gather(d_out, "head", axis=0, tiled=True),
        out_weight,
        (((1,), (1,)), ((), ())),
        preferred_element_type=jnp.float32,
    ).astype(jnp.bfloat16)
    keys_all, values_all, episode_all = (
        lax.all_gather(keys, "ctx", axis=0, tiled=True),
        lax.all_gather(values, "ctx", axis=0, tiled=True),
        lax.all_gather(episode, "ctx", axis=0, tiled=True),
    )
    total = keys_all.shape[0]
    query_pos = place * rows_local + jnp.arange(rows_local, dtype=jnp.int32)
    query_time = time_steps(query_pos, rows_local, ctx_count)
    key_time = time_steps(jnp.arange(total, dtype=jnp.int32), rows_local, ctx_count)
    visible = (key_time[None, :] <= query_time[:, None]) & (
        episode[:, None] - episode_all[None, :] < window
    )
    query_heads = queries.reshape(rows_local, heads, HD)
    key_heads = keys_all.reshape(total, heads, HD)
    value_heads = values_all.reshape(total, heads, HD)
    scores = (
        jnp.einsum("qhd,khd->hqk", query_heads, key_heads, preferred_element_type=jnp.float32)
        * scale
    )
    scores = jnp.where(visible[None], scores, floor_score)
    top = jnp.max(scores, axis=2)
    lse = top + jnp.log(jnp.sum(jnp.exp(scores - top[:, :, None]), axis=2))
    probs = jnp.exp(scores - lse[:, :, None])
    probs_low = probs.astype(jnp.bfloat16)
    attn_heads = jnp.einsum(
        "hqk,khd->qhd", probs_low, value_heads, preferred_element_type=jnp.float32
    ).astype(jnp.bfloat16)
    attn = attn_heads.reshape(rows_local, width)
    mixed = lax.psum_scatter(
        jnp.dot(attn, out_weight, preferred_element_type=jnp.float32),
        "head",
        scatter_dimension=0,
        tiled=True,
    ).astype(jnp.bfloat16)
    d_heads = d_attn.reshape(rows_local, heads, HD)
    delta = jnp.sum(d_heads.astype(jnp.float32) * attn_heads.astype(jnp.float32), axis=2).T
    d_probs = jnp.einsum("qhd,khd->hqk", d_heads, value_heads, preferred_element_type=jnp.float32)
    d_scores = (probs * (d_probs - delta[:, :, None])).astype(jnp.bfloat16)
    dq_sum = jnp.einsum("hqk,khd->qhd", d_scores, key_heads, preferred_element_type=jnp.float32)
    d_queries = (scale * dq_sum).astype(jnp.bfloat16).reshape(rows_local, width)
    lse_all, delta_all = (
        lax.all_gather(lse.T, "ctx", axis=0, tiled=True),
        lax.all_gather(delta.T, "ctx", axis=0, tiled=True),
    )
    own_keys = keys.reshape(rows_local, heads, HD)
    own_values = values.reshape(rows_local, heads, HD)
    piece_q = lax.all_gather(queries, "ctx", axis=0, tiled=True)
    piece_d = lax.all_gather(d_attn, "ctx", axis=0, tiled=True)
    piece_ep = lax.all_gather(episode, "ctx", axis=0, tiled=True)
    count = piece_q.shape[0]
    piece_qh = piece_q.reshape(count, heads, HD)
    piece_dh = piece_d.reshape(count, heads, HD)
    piece_pos = jnp.arange(count, dtype=jnp.int32)
    piece_time = time_steps(piece_pos, rows_local, ctx_count)
    piece_mask = (query_time[None, :] <= piece_time[:, None]) & (
        piece_ep[:, None] - episode[None, :] < window
    )
    piece_scores = (
        jnp.einsum("qhd,khd->hqk", piece_qh, own_keys, preferred_element_type=jnp.float32) * scale
    )
    piece_scores = jnp.where(piece_mask[None], piece_scores, floor_score)
    piece_lse = lse_all.T
    piece_delta = delta_all.T
    piece_probs = jnp.exp(piece_scores - piece_lse[:, :, None])
    piece_dprobs = jnp.einsum(
        "qhd,khd->hqk", piece_dh, own_values, preferred_element_type=jnp.float32
    )
    piece_ds = (piece_probs * (piece_dprobs - piece_delta[:, :, None])).astype(jnp.bfloat16)
    dk_sum = jnp.einsum("hqk,qhd->khd", piece_ds, piece_qh, preferred_element_type=jnp.float32)
    dv_sum = jnp.einsum(
        "hqk,qhd->khd",
        piece_probs.astype(jnp.bfloat16),
        piece_dh,
        preferred_element_type=jnp.float32,
    )
    d_keys = (scale * dk_sum).astype(jnp.bfloat16).reshape(rows_local, width)
    d_values = dv_sum.astype(jnp.bfloat16).reshape(rows_local, width)
    return (mixed, d_queries, d_keys, d_values)


def by_head(array, heads):
    rows_local = array.shape[0]
    return array.reshape(rows_local, heads, HD).transpose(1, 0, 2)


def on_device_heads(queries, keys, values, episode, out_weight, d_out):
    rows_local, width = queries.shape
    heads = width // HD
    scale = HD ** (-0.5)
    ctx_count = lax.axis_size("ctx")
    head_count = lax.axis_size("head")
    own = heads // ctx_count
    total = rows_local * ctx_count
    window = 2 * ctx_count

    def spread(arrays):
        parts = [by_head(a, heads).reshape(ctx_count, own, rows_local, HD) for a in arrays]
        got = lax.all_to_all(jnp.stack(parts, 1), "ctx", 0, 0, tiled=True)
        return [got[:, i].transpose(1, 0, 2, 3).reshape(own, total, HD) for i in range(len(arrays))]

    def collect(arrays):
        parts = [a.reshape(own, ctx_count, rows_local, HD).transpose(1, 0, 2, 3) for a in arrays]
        got = lax.all_to_all(jnp.stack(parts, 1), "ctx", 0, 0, tiled=True)
        return [
            got[:, i].reshape(heads, rows_local, HD).transpose(1, 0, 2).reshape(rows_local, width)
            for i in range(len(arrays))
        ]

    d_all = lax.all_gather(d_out, "head", axis=0, tiled=True)
    episode_all = lax.all_gather(episode, "ctx", axis=0, tiled=True)
    q, k, v = spread([queries, keys, values])
    d_attn = lax.dot_general(
        d_all, out_weight, (((1,), (1,)), ((), ())), preferred_element_type=jnp.float32
    ).astype(jnp.bfloat16)
    (da,) = spread([d_attn])

    time = time_steps(jnp.arange(total, dtype=jnp.int32), rows_local, ctx_count)
    visible = (time[None, :] <= time[:, None]) & (
        episode_all[:, None] - episode_all[None, :] < window
    )
    scores = jnp.einsum("hqd,hkd->hqk", q, k, preferred_element_type=jnp.float32) * scale
    scores = jnp.where(visible[None], scores, floor_score)
    top = jnp.max(scores, axis=2)
    lse = top + jnp.log(jnp.sum(jnp.exp(scores - top[:, :, None]), axis=2))
    probs = jnp.exp(scores - lse[:, :, None])
    probs_low = probs.astype(jnp.bfloat16)
    attn = jnp.einsum("hqk,hkd->hqd", probs_low, v, preferred_element_type=jnp.float32).astype(
        jnp.bfloat16
    )
    (attn_rows,) = collect([attn])
    delta = jnp.sum(da.astype(jnp.float32) * attn.astype(jnp.float32), axis=2)
    d_probs = jnp.einsum("hqd,hkd->hqk", da, v, preferred_element_type=jnp.float32)
    d_scores = (probs * (d_probs - delta[:, :, None])).astype(jnp.bfloat16)
    dq = jnp.einsum("hqk,hkd->hqd", d_scores, k, preferred_element_type=jnp.float32)
    dk = jnp.einsum("hqk,hqd->hkd", d_scores, q, preferred_element_type=jnp.float32)
    dv = jnp.einsum("hqk,hqd->hkd", probs_low, da, preferred_element_type=jnp.float32)
    d_queries, d_keys, d_values = collect(
        [
            (scale * dq).astype(jnp.bfloat16),
            (scale * dk).astype(jnp.bfloat16),
            dv.astype(jnp.bfloat16),
        ]
    )
    share = jnp.dot(attn_rows, out_weight, preferred_element_type=jnp.float32).astype(jnp.bfloat16)
    share = share.reshape(head_count, rows_local // head_count, share.shape[1])
    shares = lax.all_to_all(share, "head", 0, 0, tiled=True)
    mixed = jnp.sum(shares.astype(jnp.float32), axis=0).astype(jnp.bfloat16)
    return (mixed, d_queries, d_keys, d_values)


def route(queries, keys, values, episode, out_weight, d_out):
    heads = queries.shape[1] // HD
    if heads % lax.axis_size("ctx") == 0:
        return on_device_heads(queries, keys, values, episode, out_weight, d_out)
    return on_device(queries, keys, values, episode, out_weight, d_out)


def solution(mesh):
    placed = (
        P("ctx", "head"),
        P("ctx", "head"),
        P("ctx", "head"),
        P("ctx"),
        P("head", None),
        P(("ctx", "head"), None),
    )
    return jax.shard_map(
        route,
        mesh=mesh,
        in_specs=placed,
        out_specs=(P(("ctx", "head"), None), P("ctx", "head"), P("ctx", "head"), P("ctx", "head")),
        check_vma=False,
    )
```
